256 devices in a mesh: dp: 32 (over x_lo, z, core), tensor: 8 (over y, x_hi).
Axes of the slice: x: 4 (x_hi: 2, x_lo: 2; x = x_hi * 2 + x_lo), y: 4, z: 8, core: 2. Of those that a mesh axis runs over, the one named last changes fastest.
Arguments:
- hidden: bfloat16 [8192, 18432], P('dp', 'tensor'), may hold values from -6 to 6
- down_weight: bfloat16 [18432, 2304], P('tensor', 'dp'), may hold values from -0.046875 to 0.046875
- norm_gain: float32 [2304], replicated, may hold values from 0.25 to 1.75
- teacher: bfloat16 [8192, 2304], P(('dp', 'tensor')), may hold values from -6 to 6
- error_memory: bfloat16 [32, 18432, 2304], P('dp', 'tensor'), may hold values from -0.59765625 to 0.59765625
- start_basis: bfloat16 [2304, 64], replicated, may hold values from -6 to 6
Outputs:
- normed: bfloat16 [8192, 2304], P(('dp', 'tensor'))
- left_basis: bfloat16 [18432, 64], P('tensor')
- right_factor: bfloat16 [2304, 64], replicated
The draws below stay inside these ranges and needn't reach their ends.
All inputs are finite; a program needn't handle non-finite values.
Results may differ from the reference program's by a relative error of at most 0.0075.
Values may be sent and summed in bfloat16 or wider, within the bound.
No kernel may reach another device: no remote copies, remote signals or barrier semaphores. Data moves between devices by JAX's collectives and lax.ppermute only.
A program may use at most 128 MiB of HBM per device.

```python
import math
import jax
import jax.numpy as jnp
from jax import lax

D = 2304
FF = 18432
R = 64
TOK_DEV = 256
WORKERS = 32
TOKENS = 8192


def with_spikes(values, key, source, target, parts, factor):
    def block_of(position):
        return (jnp.arange(values.shape[position]) // (values.shape[position] // parts)).reshape((-1,) + (1,) * (values.ndim - 1 - position))

    near = jax.random.permutation(key, parts)[block_of(target)]
    second = (block_of(target) + parts // 2) % parts
    return jnp.where((block_of(source) == near) | (block_of(source) == second), factor * values, values)


def shard_levels(key, extent, pieces, smallest, high):
    gain = 1.0
    for position, shards_of in pieces:
        steps = jax.random.uniform(jax.random.fold_in(jax.random.fold_in(key, 6), position), (shards_of,), jnp.float32, smallest / len(pieces), high / len(pieces))
        gain = gain * jnp.repeat(jnp.exp(steps), extent[position] // shards_of).reshape((-1,) + (1,) * (len(extent) - 1 - position))
    return gain


def bell_draw(key, extent, deviation, reach, split=(), held_as=jnp.bfloat16):
    drawn = jax.random.normal(key, extent, jnp.float32) * deviation
    if len(split) > 0:
        drawn = shard_levels(key, extent, split, -0.22, 0.18) * drawn
    return jnp.clip(drawn, min=-reach, max=reach).astype(held_as)


def heavy_noise(rng, extent, spread, limit, pieces, heavy, dtype=jnp.bfloat16):
    result = spread * jax.random.normal(rng, extent, jnp.float32)
    if pieces:
        result = result * shard_levels(rng, extent, pieces, -0.22, 0.18)
    return jnp.clip(with_spikes(result, jax.random.fold_in(rng, 3), *heavy), -limit, limit).astype(dtype)


def setup_inputs(seed: int = 0) -> dict:
    arg_keys = jax.random.split(jax.random.key(seed), 7)
    hidden = bell_draw(arg_keys[0], (TOKENS, FF), 1.0, 6.0, ((0, 32), (1, 8)))
    down_weight = bell_draw(arg_keys[1], (FF, D), FF ** -0.5, 0.046875, ((0, 8), (1, 32)))
    norm_gain = jnp.clip(1.0 + 0.15 * jax.random.normal(arg_keys[2], (D,), jnp.float32), 0.25, 1.75)
    teacher = bell_draw(arg_keys[3], (TOKENS, D), 1.0, 6.0, ((0, 256),))
    error_memory = heavy_noise(arg_keys[4], (WORKERS, FF, D), 0.1, 0.59765625, ((0, 32), (1, 8)), (0, 2, 32, 2.75))
    start_basis = bell_draw(arg_keys[5], (D, R), 1.0, 6.0)
    return dict(hidden=hidden, down_weight=down_weight, norm_gain=norm_gain, teacher=teacher, error_memory=error_memory, start_basis=start_basis)


def reference(hidden, down_weight, norm_gain, teacher, error_memory, start_basis):
    mixed = jnp.dot(hidden.astype(jnp.float32), down_weight.astype(jnp.float32), preferred_element_type=jnp.float32)
    scale = lax.rsqrt(lax.optimization_barrier(jnp.mean(mixed * mixed, axis=1, keepdims=True)) + 1e-06)
    unit = mixed * scale
    normed_full = unit * norm_gain
    normed = normed_full.astype(jnp.bfloat16)
    diff = normed_full - teacher.astype(jnp.float32)
    delta = diff / TOK_DEV * norm_gain
    grad_f = scale * (delta - unit * lax.optimization_barrier(jnp.mean(delta * unit, axis=1, keepdims=True)))
    grad_out = grad_f.astype(jnp.bfloat16)
    hidden_w = hidden.reshape(WORKERS, TOK_DEV, FF)
    grad_w = grad_out.reshape(WORKERS, TOK_DEV, D)

    def left_step(total, items):
        hid, grd, memory = items
        probe = jnp.dot(grd.astype(jnp.float32), start_basis.astype(jnp.float32), preferred_element_type=jnp.float32).astype(jnp.bfloat16)
        term = lax.dot_general(hid.astype(jnp.float32), probe.astype(jnp.float32), (((0,), (0,)), ((), ())), preferred_element_type=jnp.float32)
        term = term + jnp.dot(memory.astype(jnp.float32), start_basis.astype(jnp.float32), preferred_element_type=jnp.float32)
        return (total + term, None)
    left_sum, _ = lax.scan(left_step, jnp.zeros((FF, R), jnp.float32), (hidden_w, grad_w, error_memory))
    gram = jnp.dot(left_sum.T, left_sum, precision=lax.Precision.HIGHEST)
    lower = jnp.linalg.cholesky(gram)
    solved = lax.linalg.triangular_solve(lower, left_sum, left_side=False, lower=True, transpose_a=True)
    left_basis = (solved * math.sqrt(FF)).astype(jnp.bfloat16)

    def right_step(total, items):
        hid, grd, memory = items
        image = jnp.dot(hid.astype(jnp.float32), left_basis.astype(jnp.float32), preferred_element_type=jnp.float32).astype(jnp.bfloat16)
        term = lax.dot_general(grd.astype(jnp.float32), image.astype(jnp.float32), (((0,), (0,)), ((), ())), preferred_element_type=jnp.float32)
        term = term + lax.dot_general(memory.astype(jnp.float32), left_basis.astype(jnp.float32), (((0,), (0,)), ((), ())), preferred_element_type=jnp.float32)
        return (total + term, None)
    right_total, _ = lax.scan(right_step, jnp.zeros((D, R), jnp.float32), (hidden_w, grad_w, error_memory))
    right_factor = (right_total / math.sqrt(FF)).astype(jnp.bfloat16)
    return (normed, left_basis, right_factor)
```

```python
import math

import jax
import jax.numpy as jnp
from jax import lax
from jax.sharding import Mesh
from jax.sharding import PartitionSpec as P

DP = ("xl", "z", "c")
TENSOR = ("y", "xh")
SWAP = [(0, 1), (1, 0)]
F32 = jnp.float32
BF16 = jnp.bfloat16


def dot(a, b, dims, precision=None):
    return lax.dot_general(a, b, (dims, ((), ())), precision=precision, preferred_element_type=F32)


def split_bf16(x):
    high = lax.reduce_precision(x, 8, 7)
    low = x - high
    return jnp.concatenate([high.astype(BF16), low.astype(BF16)], axis=0)


def share_out(x, axes):
    n = lax.axis_size(axes)
    return lax.all_to_all(jnp.broadcast_to(x[None], (n,) + x.shape), axes, 0, 0)


def pair(x, axis):
    other = lax.ppermute(x, axis, SWAP)
    first = lax.axis_index(axis) == 0
    return jnp.where(first, jnp.stack([x, other]), jnp.stack([other, x]))


def sum_pair_halves(x, axis):
    half = x.shape[-1] // 2
    first = lax.axis_index(axis) == 0
    mine = jnp.where(first, x[..., :half], x[..., half:])
    theirs = jnp.where(first, x[..., half:], x[..., :half])
    return mine + lax.ppermute(theirs, axis, SWAP)


def per_device(hidden, down_weight, norm_gain, teacher, error_memory, start_basis):
    memory = error_memory[0]
    tokens, units = hidden.shape
    feats, rank = start_basis.shape
    block = down_weight.shape[1]
    n_z = lax.axis_size("z")
    n_t = lax.axis_size(TENSOR)
    share = tokens // n_t
    all_units = units * n_t

    columns = lax.all_gather(down_weight.T, "z", axis=0, tiled=True)
    rows = pair(hidden, "xl")
    rows = jnp.swapaxes(pair(rows, "c"), 0, 1)
    partial_out = dot(rows.reshape(4 * tokens, units), columns, ((1,), (1,))).astype(BF16)
    parts = lax.all_to_all(
        partial_out.reshape(4 * n_t, share, n_z * block), ("xl", "c") + TENSOR, 0, 0
    )
    mixed = jnp.sum(parts.reshape(2, 2, n_t, share, n_z, block).astype(F32), axis=2)
    mixed = jnp.transpose(mixed, (2, 0, 3, 1, 4)).reshape(share, feats)

    scale = lax.rsqrt(jnp.mean(mixed * mixed, axis=1, keepdims=True) + 1e-06)
    unit = mixed * scale
    normed_full = unit * norm_gain
    delta = (normed_full - teacher.astype(F32)) / tokens * norm_gain
    grad = (scale * (delta - unit * jnp.mean(delta * unit, axis=1, keepdims=True))).astype(BF16)
    normed = normed_full.astype(BF16)
    grad_all = lax.all_gather(grad, TENSOR, axis=0, tiled=True)

    probe = dot(grad, start_basis, ((1,), (0,))).astype(BF16)
    probe_all = share_out(probe, TENSOR).reshape(tokens, rank)
    term = dot(start_basis, memory, ((0,), (1,))) + dot(probe_all, hidden, ((0,), (0,)))
    half = sum_pair_halves(term, "c")
    pieces = lax.all_to_all(half.reshape(2 * n_z, rank // (2 * n_z), units // 2), ("xl", "z"), 0, 0)
    piece = jnp.sum(pieces, axis=0)
    half = share_out(piece, ("xl", "z")).reshape(rank, units // 2)
    left = jnp.transpose(pair(half, "c"), (1, 0, 2)).reshape(rank, units)

    left2 = split_bf16(left)
    gram = dot(left, left, ((1,), (1,)), lax.Precision.HIGHEST)
    image = dot(left2, hidden, ((1,), (1,)))
    image = image[:rank] + image[rank:]
    pulled = dot(left2, memory, ((1,), (0,)))
    pulled = pulled[:rank] + pulled[rank:]
    lines = rank // n_t
    message = jnp.concatenate(
        [
            pulled.reshape(n_t, lines, feats),
            image.reshape(n_t, lines, tokens),
            jnp.broadcast_to(gram.reshape(1, lines, n_t * rank), (n_t, lines, n_t * rank)),
        ],
        axis=2,
    )
    message = jnp.sum(lax.all_to_all(message, TENSOR, 0, 0), axis=0)
    pulled = message[:, :feats]
    image = message[:, feats : feats + tokens]
    gram = message[:, feats + tokens :].reshape(rank, rank)

    right = dot(split_bf16(image), grad_all, ((1,), (0,)))
    right = right[:lines] + right[lines:] + pulled
    right = jnp.sum(share_out(sum_pair_halves(right, "c"), ("xl", "z")), axis=0)
    right = share_out(right, ("c",) + TENSOR)
    right = jnp.transpose(right.reshape(2, rank, feats // 2), (1, 0, 2)).reshape(rank, feats)

    lower = jnp.linalg.cholesky(gram)
    inverse = lax.linalg.triangular_solve(lower, jnp.eye(rank, dtype=F32), left_side=True, lower=True)
    left_basis = dot(left, inverse, ((0,), (1,)), lax.Precision.HIGHEST) * math.sqrt(all_units)
    right_factor = dot(right, inverse, ((0,), (1,)), lax.Precision.HIGHEST)
    return normed, left_basis.astype(BF16), right_factor.astype(BF16)


def solution(mesh):
    fine = Mesh(mesh.devices.reshape(2, 8, 2, 4, 2), DP + TENSOR)
    in_specs = (
        P(DP, TENSOR),
        P(TENSOR, DP),
        P(),
        P(DP + TENSOR, None),
        P(DP, TENSOR, None),
        P(),
    )
    out_specs = (P(DP + TENSOR, None), P(TENSOR, None), P())
    return jax.shard_map(
        per_device, mesh=fine, in_specs=in_specs, out_specs=out_specs, check_vma=False
    )
```

```python
import functools
import math

import jax
import jax.numpy as jnp
from jax import lax
from jax.experimental import pallas as pl
from jax.experimental.pallas import tpu as pltpu
from jax.sharding import Mesh
from jax.sharding import PartitionSpec as P

DP = ("xl", "z", "c")
TENSOR = ("y", "xh")
SWAP = [(0, 1), (1, 0)]
F32 = jnp.float32
BF16 = jnp.bfloat16


def dot(a, b, dims, precision=None):
    return lax.dot_general(a, b, (dims, ((), ())), precision=precision, preferred_element_type=F32)


def split_bf16(x):
    high = lax.reduce_precision(x, 8, 7)
    low = x - high
    return jnp.concatenate([high.astype(BF16), low.astype(BF16)], axis=0)


def share_out(x, axes):
    n = lax.axis_size(axes)
    return lax.all_to_all(jnp.broadcast_to(x[None], (n,) + x.shape), axes, 0, 0)


def pair(x, axis):
    other = lax.ppermute(x, axis, SWAP)
    first = lax.axis_index(axis) == 0
    return jnp.concatenate([jnp.where(first, x, other), jnp.where(first, other, x)], axis=0)


def sum_pair_halves(x, axis, dim):
    low, high = jnp.split(x, 2, axis=dim)
    first = lax.axis_index(axis) == 0
    return jnp.where(first, low, high) + lax.ppermute(jnp.where(first, high, low), axis, SWAP)


def shift(x, axis, by):
    n = lax.axis_size(axis)
    return lax.ppermute(x, axis, [(i, (i + by) % n) for i in range(n)])


def columns_kernel(me_ref, *refs):
    *sources, out_ref, rows, blocks, columns, row_sems, block_sems = refs
    n_z, block, units = blocks.shape
    cut = rows.shape[1] // 4
    targets = [rows.at[k] for k in range(3)] + [rows.at[3, k * cut : (k + 1) * cut] for k in range(4)]
    targets += [blocks.at[k] for k in range(n_z) if k != n_z // 2]
    targets += [blocks.at[n_z // 2, :, : units // 2], blocks.at[n_z // 2, :, units // 2 :]]
    sems = [row_sems.at[k] for k in range(7)] + [block_sems.at[k] for k in range(n_z + 1)]
    copies = [pltpu.make_async_copy(*args) for args in zip(sources, targets, sems)]
    for copy in copies[7:] + copies[:7]:
        copy.start()
    for copy in copies[7:]:
        copy.wait()
    for k in range(n_z):
        columns[k * block : (k + 1) * block, :] = blocks[k]
    for k in range(4):
        for copy in copies[k : k + 1] if k < 3 else copies[3:7]:
            copy.wait()
        out_ref[me_ref[0] ^ k] = dot(rows[k], columns[...], ((1,), (1,))).astype(BF16)


def column_products(rows, blocks):
    tokens, units = rows[0].shape
    block = blocks[0].shape[0]
    n_z = lax.axis_size("z")
    me = 2 * lax.axis_index("xl") + lax.axis_index("c")
    return pl.pallas_call(
        columns_kernel,
        out_shape=jax.ShapeDtypeStruct((4, tokens, n_z * block), BF16),
        in_specs=[pl.BlockSpec(memory_space=pltpu.SMEM)]
        + [pl.BlockSpec(memory_space=pl.ANY)] * (len(rows) + len(blocks)),
        out_specs=pl.BlockSpec(memory_space=pltpu.VMEM),
        scratch_shapes=[
            pltpu.VMEM((4, tokens, units), BF16),
            pltpu.VMEM((n_z, block, units), BF16),
            pltpu.VMEM((n_z * block, units), BF16),
            pltpu.SemaphoreType.DMA((7,)),
            pltpu.SemaphoreType.DMA((n_z + 1,)),
        ],
        compiler_params=pltpu.CompilerParams(vmem_limit_bytes=56 * 2**20),
    )(me.reshape(1), *rows, *blocks)


def norm_kernel(z_ref, parts_ref, gain_ref, teacher_ref, basis_ref, normed_ref, sent_ref, blocks, mixed_ref, *, tokens):
    n_z, _, _, two = blocks.shape
    block = two // 2
    share, feats = mixed_ref.shape
    n_t = parts_ref.shape[0] // 4
    for x in range(2):
        for c in range(2):
            total = jnp.zeros((share, n_z * block), F32)
            for t in range(n_t):
                total += parts_ref[(2 * x + c) * n_t + t].astype(F32)
            for k in range(n_z):
                blocks[k, x, :, c * block : (c + 1) * block] = total[:, k * block : (k + 1) * block]
    for x in range(2):
        for z in range(n_z):
            at = (x * n_z + z) * two
            mixed_ref[:, at : at + two] = blocks[lax.rem(z - z_ref[0] + n_z, n_z), x]
    mixed = mixed_ref[...]
    gain = gain_ref[...]
    scale = lax.rsqrt(jnp.mean(mixed * mixed, axis=1, keepdims=True) + 1e-06)
    unit = mixed * scale
    normed_full = unit * gain
    normed_ref[...] = normed_full.astype(BF16)
    delta = (normed_full - teacher_ref[...].astype(F32)) * (gain / tokens)
    grad = (scale * (delta - unit * jnp.mean(delta * unit, axis=1, keepdims=True))).astype(BF16)
    probe = dot(grad, basis_ref[...], ((1,), (1,))).astype(BF16)
    for t in range(n_t):
        sent_ref[t, :, :feats] = grad
        sent_ref[t, :, feats:] = probe


def norm_head(parts, norm_gain, teacher, basis_t, tokens):
    share, feats = teacher.shape
    n_z = lax.axis_size("z")
    n_t = parts.shape[0] // 4
    vmem = pl.BlockSpec(memory_space=pltpu.VMEM)
    return pl.pallas_call(
        functools.partial(norm_kernel, tokens=tokens),
        out_shape=(
            jax.ShapeDtypeStruct((share, feats), BF16),
            jax.ShapeDtypeStruct((n_t, share, feats + basis_t.shape[0]), BF16),
        ),
        in_specs=[pl.BlockSpec(memory_space=pltpu.SMEM)] + [vmem] * 4,
        out_specs=(vmem, vmem),
        scratch_shapes=[
            pltpu.VMEM((n_z, 2, share, feats // (2 * n_z)), F32),
            pltpu.VMEM((share, feats), F32),
        ],
        compiler_params=pltpu.CompilerParams(vmem_limit_bytes=32 * 2**20),
    )(lax.axis_index("z").reshape(1), parts, norm_gain.reshape(1, feats), teacher, basis_t)


def per_device(hidden, down_weight, norm_gain, teacher, error_memory, start_basis):
    memory = error_memory[0]
    tokens, units = hidden.shape
    feats, rank = start_basis.shape
    block = down_weight.shape[1]
    n_z = lax.axis_size("z")
    n_t = lax.axis_size(TENSOR)
    share = tokens // n_t
    all_units = units * n_t

    block_t = down_weight.T
    x_other = lax.ppermute(hidden, "xl", SWAP)
    c_other = lax.ppermute(hidden, "c", SWAP)
    both = [lax.ppermute(x, "c", SWAP) for x in jnp.split(x_other, 4, axis=0)]
    up, down = [block_t], [block_t]
    for _ in range(n_z // 2 - 1):
        up.append(shift(up[-1], "z", 1))
        down.append(shift(down[-1], "z", -1))
    memory_term = dot(start_basis, memory, ((0,), (1,)))
    near = shift(up[-1][:, : units // 2], "z", 1)
    far = shift(down[-1][:, units // 2 :], "z", -1)
    rows = (hidden, c_other, x_other, *both)
    pieces = column_products(rows, down + up[:0:-1] + [near, far])
    pieces = pieces.reshape(4 * n_t, share, n_z * block)
    parts = lax.all_to_all(pieces, ("xl", "c") + TENSOR, 0, 0)
    parts, memory_term = lax.optimization_barrier((parts, memory_term))

    normed, sent = norm_head(parts, norm_gain, teacher, start_basis.T, tokens)
    sent = lax.all_to_all(sent, TENSOR, 0, 0)
    grad = sent[:, :, :feats].reshape(tokens, feats)
    probe = sent[:, :, feats:].reshape(tokens, rank)

    term = memory_term + dot(probe, hidden, ((0,), (0,)))
    half = sum_pair_halves(term, "c", 0)
    pieces = lax.all_to_all(half.reshape(2 * n_z, rank // (4 * n_z), units), ("xl", "z"), 0, 0)
    piece = jnp.sum(pieces, axis=0)
    left = pair(share_out(piece, ("xl", "z")).reshape(rank // 2, units), "c")

    left2 = split_bf16(left)
    gram = dot(left, left, ((1,), (1,)), lax.Precision.HIGHEST)
    image = dot(left2, hidden, ((1,), (1,)))
    image = split_bf16(image[:rank] + image[rank:])
    right = dot(image, grad, ((1,), (0,))) + dot(left2, memory, ((1,), (0,)))
    right = right[:rank] + right[rank:]

    right = sum_pair_halves(sum_pair_halves(right, "c", 0), "xl", 0)
    lines = right.shape[0] // n_t
    gram = jnp.broadcast_to(gram.reshape(1, lines, -1), (n_t, lines, rank * rank // lines))
    message = jnp.concatenate([right.reshape(n_t, lines, feats), gram], axis=2)
    message = jnp.sum(lax.all_to_all(message, TENSOR, 0, 0), axis=0)
    gram = message[:, feats:].reshape(rank, rank)
    right = jnp.sum(share_out(message[:, :feats], "z"), axis=0)
    right = share_out(right, ("c", "xl") + TENSOR).reshape(rank, feats)

    lower = jnp.linalg.cholesky(gram)
    inverse = lax.linalg.triangular_solve(lower, jnp.eye(rank, dtype=F32), left_side=True, lower=True)
    left_basis = dot(left, inverse, ((0,), (1,)), lax.Precision.HIGHEST) * math.sqrt(all_units)
    right_factor = dot(right, inverse, ((0,), (1,)), lax.Precision.HIGHEST)
    return normed, left_basis.astype(BF16), right_factor.astype(BF16)


def solution(mesh):
    fine = Mesh(mesh.devices.reshape(2, 8, 2, 4, 2), DP + TENSOR)
    in_specs = (
        P(DP, TENSOR),
        P(TENSOR, DP),
        P(),
        P(DP + TENSOR, None),
        P(DP, TENSOR, None),
        P(),
    )
    out_specs = (P(DP + TENSOR, None), P(TENSOR, None), P())
    return jax.shard_map(
        per_device, mesh=fine, in_specs=in_specs, out_specs=out_specs, check_vma=False
    )
```

```python
import functools
import math

import jax
import jax.numpy as jnp
from jax import lax
from jax.experimental import pallas as pl
from jax.experimental.pallas import tpu as pltpu
from jax.sharding import Mesh
from jax.sharding import PartitionSpec as P

DP = ("xl", "z", "c")
TENSOR = ("y", "xh")
SWAP = [(0, 1), (1, 0)]
F32 = jnp.float32
BF16 = jnp.bfloat16


def dot(a, b, dims, precision=None):
    return lax.dot_general(a, b, (dims, ((), ())), precision=precision, preferred_element_type=F32)


def split_bf16(x):
    high = lax.reduce_precision(x, 8, 7)
    low = x - high
    return jnp.concatenate([high.astype(BF16), low.astype(BF16)], axis=0)


def share_out(x, axes):
    n = lax.axis_size(axes)
    return lax.all_to_all(jnp.broadcast_to(x[None], (n,) + x.shape), axes, 0, 0)


def pair(x, axis):
    other = lax.ppermute(x, axis, SWAP)
    first = lax.axis_index(axis) == 0
    return jnp.concatenate([jnp.where(first, x, other), jnp.where(first, other, x)], axis=0)


def sum_pair_halves(x, axis, dim):
    low, high = jnp.split(x, 2, axis=dim)
    first = lax.axis_index(axis) == 0
    return jnp.where(first, low, high) + lax.ppermute(jnp.where(first, high, low), axis, SWAP)


def shift(x, axis, by):
    n = lax.axis_size(axis)
    return lax.ppermute(x, axis, [(i, (i + by) % n) for i in range(n)])


def ring_order(n_z):
    return [k for far in range(1, n_z // 2) for k in (far, n_z - far)] + [0, n_z // 2]


def pack_kernel(*refs):
    *blocks, out_ref = refs
    block = blocks[0].shape[0]
    for k, ref in enumerate(blocks):
        out_ref[k * block : (k + 1) * block, :] = ref[...]


def pack(blocks):
    block, units = blocks[0].shape
    vmem = pl.BlockSpec(memory_space=pltpu.VMEM)
    return pl.pallas_call(
        pack_kernel,
        out_shape=jax.ShapeDtypeStruct((len(blocks) * block, units), BF16),
        in_specs=[vmem] * len(blocks),
        out_specs=vmem,
        compiler_params=pltpu.CompilerParams(vmem_limit_bytes=16 * 2**20),
        cost_estimate=pl.CostEstimate(flops=0, bytes_accessed=4 * len(blocks) * block * units, transcendentals=0),
    )(*blocks)


def columns_kernel(me_ref, own_ref, c_ref, columns_ref, *refs):
    *sources, out_ref, x_rows, both_rows, rest, last, products, sems, out_sems = refs
    width = columns_ref.shape[0]
    tokens, units = own_ref.shape
    block = last.shape[0] // 2
    top, bottom = pl.ds(0, tokens // 2), pl.ds(tokens // 2, tokens // 2)
    left, right = pl.ds(0, units // 2), pl.ds(units // 2, units // 2)
    targets = [rest.at[0], rest.at[1, :, left], rest.at[1, :, right]]
    targets += [x_rows, both_rows.at[top, :], both_rows.at[bottom, :]]
    brought = [pltpu.make_async_copy(x, y, sems.at[k]) for k, (x, y) in enumerate(zip(sources, targets))]
    for copy in brought:
        copy.start()
    sent = []

    def main(k, ref):
        products[k, :, :width] = dot(ref[...], columns_ref[...], ((1,), (1,))).astype(BF16)

    def finish(k, ref):
        products[k, :, width:] = dot(ref[...], last[...], ((1,), (1,))).astype(BF16)
        sent.append(pltpu.make_async_copy(products.at[k], out_ref.at[me_ref[0] ^ k], out_sems.at[k]))
        sent[-1].start()

    main(0, own_ref)
    for copy in brought[:3]:
        copy.wait()
    last[:block, :] = rest[0]
    last[block:, :] = rest[1]
    finish(0, own_ref)
    main(1, c_ref)
    finish(1, c_ref)
    brought[3].wait()
    main(2, x_rows)
    finish(2, x_rows)
    for copy in brought[4:]:
        copy.wait()
    main(3, both_rows)
    finish(3, both_rows)
    for copy in sent:
        copy.wait()


def column_products(rows, columns, rest, halves):
    tokens, units = rows[0].shape
    block = rest[0].shape[0]
    me = 2 * lax.axis_index("xl") + lax.axis_index("c")
    out = jax.ShapeDtypeStruct((4, tokens, columns.shape[0] + 2 * block), BF16)
    vmem = pl.BlockSpec(memory_space=pltpu.VMEM)
    hbm = pl.BlockSpec(memory_space=pltpu.HBM)
    return pl.pallas_call(
        columns_kernel,
        out_shape=out,
        in_specs=[pl.BlockSpec(memory_space=pltpu.SMEM)] + [vmem] * 3 + [hbm] * 6,
        out_specs=hbm,
        scratch_shapes=[
            pltpu.VMEM((tokens, units), BF16),
            pltpu.VMEM((tokens, units), BF16),
            pltpu.VMEM((2, block, units), BF16),
            pltpu.VMEM((2 * block, units), BF16),
            pltpu.VMEM(out.shape, BF16),
            pltpu.SemaphoreType.DMA((6,)),
            pltpu.SemaphoreType.DMA((4,)),
        ],
        compiler_params=pltpu.CompilerParams(vmem_limit_bytes=24 * 2**20),
    )(me.reshape(1), *rows, columns, *rest, *halves)


def norm_kernel(z_ref, parts_ref, gain_ref, teacher_ref, basis_ref, normed_ref, grad_ref, sent_ref, blocks, mixed_ref, *, tokens):
    n_z, _, _, two = blocks.shape
    block = two // 2
    share, feats = mixed_ref.shape
    n_t = parts_ref.shape[0] // 4
    for x in range(2):
        for c in range(2):
            total = jnp.zeros((share, n_z * block), F32)
            for t in range(n_t):
                total += parts_ref[(2 * x + c) * n_t + t].astype(F32)
            for at, k in enumerate(ring_order(n_z)):
                blocks[k, x, :, c * block : (c + 1) * block] = total[:, at * block : (at + 1) * block]
    for x in range(2):
        for z in range(n_z):
            at = (x * n_z + z) * two
            mixed_ref[:, at : at + two] = blocks[lax.rem(z - z_ref[0] + n_z, n_z), x]
    mixed = mixed_ref[...]
    gain = gain_ref[...]
    scale = lax.rsqrt(jnp.mean(mixed * mixed, axis=1, keepdims=True) + 1e-06)
    unit = mixed * scale
    normed_full = unit * gain
    normed_ref[...] = normed_full.astype(BF16)
    delta = (normed_full - teacher_ref[...].astype(F32)) * (gain / tokens)
    grad = (scale * (delta - unit * jnp.mean(delta * unit, axis=1, keepdims=True))).astype(BF16)
    grad_ref[...] = grad
    probe = dot(grad, basis_ref[...], ((1,), (1,))).astype(BF16)
    for t in range(n_t):
        sent_ref[t] = probe


def norm_head(parts, norm_gain, teacher, basis_t, tokens):
    share, feats = teacher.shape
    n_z = lax.axis_size("z")
    n_t = parts.shape[0] // 4
    vmem = pl.BlockSpec(memory_space=pltpu.VMEM)
    return pl.pallas_call(
        functools.partial(norm_kernel, tokens=tokens),
        out_shape=(
            jax.ShapeDtypeStruct((share, feats), BF16),
            jax.ShapeDtypeStruct((share, feats), BF16),
            jax.ShapeDtypeStruct((n_t, share, basis_t.shape[0]), BF16),
        ),
        in_specs=[pl.BlockSpec(memory_space=pltpu.SMEM)] + [vmem] * 4,
        out_specs=(vmem, vmem, vmem),
        scratch_shapes=[
            pltpu.VMEM((n_z, 2, share, feats // (2 * n_z)), F32),
            pltpu.VMEM((share, feats), F32),
        ],
        compiler_params=pltpu.CompilerParams(vmem_limit_bytes=32 * 2**20),
    )(lax.axis_index("z").reshape(1), parts, norm_gain.reshape(1, feats), teacher, basis_t)


def per_device(hidden, down_weight, norm_gain, teacher, error_memory, start_basis):
    memory = error_memory[0]
    tokens, units = hidden.shape
    feats, rank = start_basis.shape
    block = down_weight.shape[1]
    n_z = lax.axis_size("z")
    n_t = lax.axis_size(TENSOR)
    share = tokens // n_t
    all_units = units * n_t

    block_t = down_weight.T
    x_other = lax.ppermute(hidden, "xl", SWAP)
    c_other = lax.ppermute(hidden, "c", SWAP)
    both = [lax.ppermute(x, "c", SWAP) for x in jnp.split(x_other, 2, axis=0)]
    up, down = [block_t], [block_t]
    for _ in range(n_z // 2 - 1):
        up.append(shift(up[-1], "z", 1))
        down.append(shift(down[-1], "z", -1))
    columns = pack([down[k] if k < n_z // 2 else up[n_z - k] for k in ring_order(n_z)[:-2]])
    near = shift(columns[-block:, : units // 2], "z", 1)
    far = shift(columns[-2 * block : -block, units // 2 :], "z", -1)
    memory_term = dot(start_basis, memory, ((0,), (1,)))
    pieces = column_products((hidden, c_other), columns, (block_t, near, far), [x_other] + both)
    pieces = pieces.reshape(4 * n_t, share, n_z * block)
    parts = lax.all_to_all(pieces, ("xl", "c") + TENSOR, 0, 0)
    parts, memory_term = lax.optimization_barrier((parts, memory_term))

    wide_basis = jnp.pad(start_basis.T, ((0, -rank % 128), (0, 0)))
    normed, grad, probe = norm_head(parts, norm_gain, teacher, wide_basis, tokens)
    probe = lax.all_to_all(probe, TENSOR, 0, 0).reshape(tokens, -1)[:, :rank]

    term = memory_term + dot(probe, hidden, ((0,), (0,)))
    half = sum_pair_halves(term, "c", 0)
    pieces = lax.all_to_all(half.reshape(2 * n_z, -1, units), ("xl", "z"), 0, 0)
    left = pair(share_out(jnp.sum(pieces, axis=0), ("xl", "z")).reshape(half.shape), "c")

    left2 = split_bf16(left)
    gram = dot(left, left, ((1,), (1,)), lax.Precision.HIGHEST)
    image = dot(hidden, left2, ((1,), (1,)))
    image = (image[:, :rank] + image[:, rank:]).reshape(n_t, share, rank)
    message = jnp.concatenate([image, jnp.broadcast_to(gram[None], (n_t, rank, rank))], axis=1)
    message = jnp.sum(lax.all_to_all(message, TENSOR, 0, 0), axis=0)
    image = split_bf16(message[:share].T)
    gram = message[share:]
    pulled = dot(left2, memory, ((1,), (0,)))
    right = dot(image, grad, ((1,), (0,))) + pulled
    right = right[:rank] + right[rank:]

    half = sum_pair_halves(right, "c", 0)
    pieces = lax.all_to_all(half.reshape(2 * n_t, -1, feats), ("xl",) + TENSOR, 0, 0)
    lower = lax.linalg.cholesky(gram, symmetrize_input=False)
    pieces = share_out(jnp.sum(pieces, axis=0), "z")
    inverse = lax.linalg.triangular_solve(lower, jnp.eye(rank, dtype=F32), left_side=True, lower=True)
    left_basis = dot(left, inverse, ((0,), (1,)), lax.Precision.HIGHEST) * math.sqrt(all_units)
    left_basis = left_basis.astype(BF16)
    half = share_out(jnp.sum(pieces, axis=0), ("xl",) + TENSOR).reshape(half.shape)
    right_factor = dot(pair(half, "c"), inverse, ((0,), (1,)), lax.Precision.HIGHEST)
    return normed, left_basis, right_factor.astype(BF16)


def solution(mesh):
    fine = Mesh(mesh.devices.reshape(2, 8, 2, 4, 2), DP + TENSOR)
    in_specs = (
        P(DP, TENSOR),
        P(TENSOR, DP),
        P(),
        P(DP + TENSOR, None),
        P(DP, TENSOR, None),
        P(),
    )
    out_specs = (P(DP + TENSOR, None), P(TENSOR, None), P())
    return jax.shard_map(
        per_device, mesh=fine, in_specs=in_specs, out_specs=out_specs, check_vma=False
    )
```

```python
import functools
import math

import jax
import jax.numpy as jnp
from jax import lax
from jax.experimental import pallas as pl
from jax.experimental.pallas import tpu as pltpu
from jax.sharding import Mesh
from jax.sharding import PartitionSpec as P

DP = ("xl", "z", "c")
TENSOR = ("y", "xh")
SWAP = [(0, 1), (1, 0)]
F32 = jnp.float32
BF16 = jnp.bfloat16


def dot(a, b, dims, precision=None):
    return lax.dot_general(a, b, (dims, ((), ())), precision=precision, preferred_element_type=F32)


def split_bf16(x):
    high = lax.reduce_precision(x, 8, 7)
    low = x - high
    return jnp.concatenate([high.astype(BF16), low.astype(BF16)], axis=0)


def share_out(x, axes):
    n = lax.axis_size(axes)
    return lax.all_to_all(jnp.broadcast_to(x[None], (n,) + x.shape), axes, 0, 0)


def pair(x, axis):
    other = lax.ppermute(x, axis, SWAP)
    first = lax.axis_index(axis) == 0
    return jnp.concatenate([jnp.where(first, x, other), jnp.where(first, other, x)], axis=0)


def sum_pair_halves(x, axis, dim):
    low, high = jnp.split(x, 2, axis=dim)
    first = lax.axis_index(axis) == 0
    return jnp.where(first, low, high) + lax.ppermute(jnp.where(first, high, low), axis, SWAP)


def shift(x, axis, by):
    n = lax.axis_size(axis)
    return lax.ppermute(x, axis, [(i, (i + by) % n) for i in range(n)])


def ring_order(n_z):
    return [0] + [k for far in range(1, n_z // 2) for k in (far, n_z - far)] + [n_z // 2]


def columns_kernel(me_ref, own_ref, c_ref, columns_ref, *refs):
    *sources, out_ref, x_rows, both_rows, last, products, sems, out_sems = refs
    width = columns_ref.shape[0]
    tokens, units = own_ref.shape
    left, right = pl.ds(0, units // 2), pl.ds(units // 2, units // 2)
    targets = [last.at[:, left], last.at[:, right]]
    targets += [x_rows]
    at = 0
    for ref in sources[3:]:
        targets.append(both_rows.at[at : at + ref.shape[0], :])
        at += ref.shape[0]
    brought = [pltpu.make_async_copy(x, y, sems.at[k]) for k, (x, y) in enumerate(zip(sources, targets))]
    for copy in brought:
        copy.start()
    sent = []

    def main(k, ref):
        products[k, :, :width] = dot(ref[...], columns_ref[...], ((1,), (1,))).astype(BF16)

    def finish(k, ref):
        products[k, :, width:] = dot(ref[...], last[...], ((1,), (1,))).astype(BF16)
        sent.append(pltpu.make_async_copy(products.at[k], out_ref.at[me_ref[0] ^ k], out_sems.at[k]))
        sent[-1].start()

    main(0, own_ref)
    for copy in brought[:2]:
        copy.wait()
    finish(0, own_ref)
    main(1, c_ref)
    finish(1, c_ref)
    brought[2].wait()
    main(2, x_rows)
    finish(2, x_rows)
    for copy in brought[3:]:
        copy.wait()
    main(3, both_rows)
    finish(3, both_rows)
    for copy in sent:
        copy.wait()


def column_products(rows, columns, rest, halves):
    tokens, units = rows[0].shape
    block = rest[0].shape[0]
    me = 2 * lax.axis_index("xl") + lax.axis_index("c")
    out = jax.ShapeDtypeStruct((4, tokens, columns.shape[0] + block), BF16)
    vmem = pl.BlockSpec(memory_space=pltpu.VMEM)
    hbm = pl.BlockSpec(memory_space=pltpu.HBM)
    return pl.pallas_call(
        columns_kernel,
        out_shape=out,
        in_specs=[pl.BlockSpec(memory_space=pltpu.SMEM)] + [vmem] * 3 + [hbm] * (len(rest) + len(halves)),
        out_specs=hbm,
        scratch_shapes=[
            pltpu.VMEM((tokens, units), BF16),
            pltpu.VMEM((tokens, units), BF16),
            pltpu.VMEM((block, units), BF16),
            pltpu.VMEM(out.shape, BF16),
            pltpu.SemaphoreType.DMA((len(rest) + len(halves),)),
            pltpu.SemaphoreType.DMA((4,)),
        ],
        compiler_params=pltpu.CompilerParams(vmem_limit_bytes=24 * 2**20),
    )(me.reshape(1), *rows, columns, *rest, *halves)


def norm_kernel(z_ref, parts_ref, gain_ref, teacher_ref, basis_ref, normed_ref, grad_ref, sent_ref, blocks, mixed_ref, *, tokens):
    n_z, _, _, two = blocks.shape
    block = two // 2
    share, feats = mixed_ref.shape
    n_t = parts_ref.shape[0] // 4
    for x in range(2):
        for c in range(2):
            total = jnp.zeros((share, n_z * block), F32)
            for t in range(n_t):
                total += parts_ref[(2 * x + c) * n_t + t].astype(F32)
            for at, k in enumerate(ring_order(n_z)):
                blocks[k, x, :, c * block : (c + 1) * block] = total[:, at * block : (at + 1) * block]
    for x in range(2):
        for z in range(n_z):
            at = (x * n_z + z) * two
            mixed_ref[:, at : at + two] = blocks[lax.rem(z - z_ref[0] + n_z, n_z), x]
    mixed = mixed_ref[...]
    gain = gain_ref[...]
    scale = lax.rsqrt(jnp.mean(mixed * mixed, axis=1, keepdims=True) + 1e-06)
    unit = mixed * scale
    normed_full = unit * gain
    normed_ref[...] = normed_full.astype(BF16)
    delta = (normed_full - teacher_ref[...].astype(F32)) * (gain / tokens)
    grad = (scale * (delta - unit * jnp.mean(delta * unit, axis=1, keepdims=True))).astype(BF16)
    grad_ref[...] = grad
    probe = dot(grad, basis_ref[...], ((1,), (1,))).astype(BF16)
    for t in range(n_t):
        sent_ref[t] = probe


def norm_head(parts, norm_gain, teacher, basis_t, tokens):
    share, feats = teacher.shape
    n_z = lax.axis_size("z")
    n_t = parts.shape[0] // 4
    vmem = pl.BlockSpec(memory_space=pltpu.VMEM)
    return pl.pallas_call(
        functools.partial(norm_kernel, tokens=tokens),
        out_shape=(
            jax.ShapeDtypeStruct((share, feats), BF16),
            jax.ShapeDtypeStruct((share, feats), BF16),
            jax.ShapeDtypeStruct((n_t, share, basis_t.shape[0]), BF16),
        ),
        in_specs=[pl.BlockSpec(memory_space=pltpu.SMEM)] + [vmem] * 4,
        out_specs=(vmem, vmem, vmem),
        scratch_shapes=[
            pltpu.VMEM((n_z, 2, share, feats // (2 * n_z)), F32),
            pltpu.VMEM((share, feats), F32),
        ],
        compiler_params=pltpu.CompilerParams(vmem_limit_bytes=32 * 2**20),
    )(lax.axis_index("z").reshape(1), parts, norm_gain.reshape(1, feats), teacher, basis_t)


def per_device(hidden, down_weight, norm_gain, teacher, error_memory, start_basis):
    memory = error_memory[0]
    tokens, units = hidden.shape
    feats, rank = start_basis.shape
    block = down_weight.shape[1]
    n_z = lax.axis_size("z")
    n_t = lax.axis_size(TENSOR)
    share = tokens // n_t
    all_units = units * n_t

    block_t = down_weight.T
    x_other = lax.ppermute(hidden, "xl", SWAP)
    c_other = lax.ppermute(hidden, "c", SWAP)
    both = [lax.ppermute(x, "c", SWAP) for x in jnp.split(x_other, 2, axis=0)]
    up, down = [block_t], [block_t]
    for _ in range(n_z // 2 - 1):
        up.append(shift(up[-1], "z", 1))
        down.append(shift(down[-1], "z", -1))
    columns = jnp.concatenate([down[k] if k < n_z // 2 else up[n_z - k] for k in ring_order(n_z)[:-1]], axis=0)
    near = shift(up[-1][:, : units // 2], "z", 1)
    far = shift(down[-1][:, units // 2 :], "z", -1)
    memory_term = dot(start_basis, memory, ((0,), (1,)))
    pieces = column_products((hidden, c_other), columns, (near, far), [x_other] + both)
    pieces = pieces.reshape(4 * n_t, share, n_z * block)
    parts = lax.all_to_all(pieces, ("xl", "c") + TENSOR, 0, 0)
    parts, memory_term = lax.optimization_barrier((parts, memory_term))

    wide_basis = jnp.pad(start_basis.T, ((0, -rank % 128), (0, 0)))
    normed, grad, probe = norm_head(parts, norm_gain, teacher, wide_basis, tokens)
    probe = lax.all_to_all(probe, TENSOR, 0, 0).reshape(tokens, -1)[:, :rank]

    term = memory_term + dot(probe, hidden, ((0,), (0,)))
    half = sum_pair_halves(term, "c", 0)
    pieces = lax.all_to_all(half.astype(BF16).reshape(2 * n_z, -1, units), ("xl", "z"), 0, 0)
    left = pair(share_out(jnp.sum(pieces.astype(F32), axis=0), ("xl", "z")).reshape(half.shape), "c")

    left2 = split_bf16(left)
    gram = dot(left, left, ((1,), (1,)), lax.Precision.HIGHEST)
    image = dot(hidden, left2, ((1,), (1,)))
    image = (image[:, :rank] + image[:, rank:]).reshape(n_t, share, rank)
    message = jnp.concatenate([image, jnp.broadcast_to(gram[None], (n_t, rank, rank))], axis=1)
    message = jnp.sum(lax.all_to_all(message, TENSOR, 0, 0), axis=0)
    image = split_bf16(message[:share].T)
    gram = message[share:]
    pulled = dot(left2, memory, ((1,), (0,)))
    right = dot(image, grad, ((1,), (0,))) + pulled
    right = right[:rank] + right[rank:]

    half = sum_pair_halves(right, "c", 0)
    pieces = lax.all_to_all(half.reshape(2 * n_t, -1, feats), ("xl",) + TENSOR, 0, 0)
    lower = lax.linalg.cholesky(gram, symmetrize_input=False)
    pieces = share_out(jnp.sum(pieces, axis=0), "z")
    inverse = lax.linalg.triangular_solve(lower, jnp.eye(rank, dtype=F32), left_side=True, lower=True)
    left_basis = dot(left, inverse, ((0,), (1,)), lax.Precision.HIGHEST) * math.sqrt(all_units)
    left_basis = left_basis.astype(BF16)
    half = share_out(jnp.sum(pieces, axis=0), ("xl",) + TENSOR).reshape(half.shape)
    right_factor = dot(pair(half, "c"), inverse, ((0,), (1,)), lax.Precision.HIGHEST)
    return normed, left_basis, right_factor.astype(BF16)


def solution(mesh):
    fine = Mesh(mesh.devices.reshape(2, 8, 2, 4, 2), DP + TENSOR)
    in_specs = (
        P(DP, TENSOR),
        P(TENSOR, DP),
        P(),
        P(DP + TENSOR, None),
        P(DP, TENSOR, None),
        P(),
    )
    out_specs = (P(DP + TENSOR, None), P(TENSOR, None), P())
    return jax.shard_map(
        per_device, mesh=fine, in_specs=in_specs, out_specs=out_specs, check_vma=False
    )
```

```python
import functools
import math

import jax
import jax.numpy as jnp
from jax import lax
from jax.experimental import pallas as pl
from jax.experimental.pallas import tpu as pltpu
from jax.sharding import Mesh
from jax.sharding import PartitionSpec as P

DP = ("xl", "z", "c")
TENSOR = ("y", "xh")
SWAP = [(0, 1), (1, 0)]
F32 = jnp.float32
BF16 = jnp.bfloat16


def dot(a, b, dims, precision=None):
    return lax.dot_general(a, b, (dims, ((), ())), precision=precision, preferred_element_type=F32)


def split_bf16(x):
    high = lax.reduce_precision(x, 8, 7)
    low = x - high
    return jnp.concatenate([high.astype(BF16), low.astype(BF16)], axis=0)


def share_out(x, axes):
    n = lax.axis_size(axes)
    return lax.all_to_all(jnp.broadcast_to(x[None], (n,) + x.shape), axes, 0, 0)


def pair(x, axis):
    other = lax.ppermute(x, axis, SWAP)
    first = lax.axis_index(axis) == 0
    return jnp.concatenate([jnp.where(first, x, other), jnp.where(first, other, x)], axis=0)


def sum_pair_halves(x, axis, dim):
    low, high = jnp.split(x, 2, axis=dim)
    first = lax.axis_index(axis) == 0
    return jnp.where(first, low, high) + lax.ppermute(jnp.where(first, high, low), axis, SWAP)


def shift(x, axis, by):
    n = lax.axis_size(axis)
    return lax.ppermute(x, axis, [(i, (i + by) % n) for i in range(n)])


def ring_order(n_z):
    return [0] + [k for far in range(1, n_z // 2) for k in (far, n_z - far)] + [n_z // 2]


def columns_kernel(me_ref, own_ref, c_ref, first_ref, second_ref, *refs):
    *sources, out_ref, x_rows, both_rows, rest, last, products, sems, out_sems = refs
    block = rest.shape[1]
    start, width = first_ref.shape[0], first_ref.shape[0] + second_ref.shape[0]
    tokens, units = own_ref.shape
    left, right = pl.ds(0, units // 2), pl.ds(units // 2, units // 2)
    targets = [rest.at[0], rest.at[1, :, left], rest.at[1, :, right]]
    targets += [x_rows]
    at = 0
    for ref in sources[4:]:
        targets.append(both_rows.at[at : at + ref.shape[0], :])
        at += ref.shape[0]
    brought = [pltpu.make_async_copy(x, y, sems.at[k]) for k, (x, y) in enumerate(zip(sources, targets))]
    for copy in brought:
        copy.start()
    sent = []

    def main(k, ref):
        products[k, :, :start] = dot(ref[...], first_ref[...], ((1,), (1,))).astype(BF16)
        products[k, :, start:width] = dot(ref[...], second_ref[...], ((1,), (1,))).astype(BF16)

    def finish(k, ref):
        products[k, :, width:] = dot(ref[...], last[...], ((1,), (1,))).astype(BF16)
        sent.append(pltpu.make_async_copy(products.at[k], out_ref.at[me_ref[0] ^ k], out_sems.at[k]))
        sent[-1].start()

    main(0, own_ref)
    for copy in brought[:3]:
        copy.wait()
    last[:block, :] = rest[0]
    last[block:, :] = rest[1]
    finish(0, own_ref)
    main(1, c_ref)
    finish(1, c_ref)
    brought[3].wait()
    main(2, x_rows)
    finish(2, x_rows)
    for copy in brought[4:]:
        copy.wait()
    main(3, both_rows)
    finish(3, both_rows)
    for copy in sent:
        copy.wait()


def column_products(rows, columns, rest, halves):
    tokens, units = rows[0].shape
    block = rest[0].shape[0]
    me = 2 * lax.axis_index("xl") + lax.axis_index("c")
    out = jax.ShapeDtypeStruct((4, tokens, sum(x.shape[0] for x in columns) + 2 * block), BF16)
    vmem = pl.BlockSpec(memory_space=pltpu.VMEM)
    hbm = pl.BlockSpec(memory_space=pltpu.HBM)
    return pl.pallas_call(
        columns_kernel,
        out_shape=out,
        in_specs=[pl.BlockSpec(memory_space=pltpu.SMEM)] + [vmem] * 4 + [hbm] * (len(rest) + len(halves)),
        out_specs=hbm,
        scratch_shapes=[
            pltpu.VMEM((tokens, units), BF16),
            pltpu.VMEM((tokens, units), BF16),
            pltpu.VMEM((2, block, units), BF16),
            pltpu.VMEM((2 * block, units), BF16),
            pltpu.VMEM(out.shape, BF16),
            pltpu.SemaphoreType.DMA((len(rest) + len(halves),)),
            pltpu.SemaphoreType.DMA((4,)),
        ],
        compiler_params=pltpu.CompilerParams(vmem_limit_bytes=24 * 2**20),
    )(me.reshape(1), *rows, *columns, *rest, *halves)


def norm_kernel(z_ref, parts_ref, gain_ref, teacher_ref, basis_ref, normed_ref, grad_ref, sent_ref, blocks, mixed_ref, *, tokens):
    n_z, _, _, two = blocks.shape
    block = two // 2
    share, feats = mixed_ref.shape
    n_t = parts_ref.shape[0] // 4
    for x in range(2):
        for c in range(2):
            total = jnp.zeros((share, n_z * block), F32)
            for t in range(n_t):
                total += parts_ref[(2 * x + c) * n_t + t].astype(F32)
            for at, k in enumerate(ring_order(n_z)):
                blocks[k, x, :, c * block : (c + 1) * block] = total[:, at * block : (at + 1) * block]
    for x in range(2):
        for z in range(n_z):
            at = (x * n_z + z) * two
            mixed_ref[:, at : at + two] = blocks[lax.rem(z - z_ref[0] + n_z, n_z), x]
    mixed = mixed_ref[...]
    gain = gain_ref[...]
    scale = lax.rsqrt(jnp.mean(mixed * mixed, axis=1, keepdims=True) + 1e-06)
    unit = mixed * scale
    normed_full = unit * gain
    normed_ref[...] = normed_full.astype(BF16)
    delta = (normed_full - teacher_ref[...].astype(F32)) * (gain / tokens)
    grad = (scale * (delta - unit * jnp.mean(delta * unit, axis=1, keepdims=True))).astype(BF16)
    grad_ref[...] = grad
    probe = dot(grad, basis_ref[...], ((1,), (1,))).astype(BF16)
    for t in range(n_t):
        sent_ref[t] = probe


def norm_head(parts, norm_gain, teacher, basis_t, tokens):
    share, feats = teacher.shape
    n_z = lax.axis_size("z")
    n_t = parts.shape[0] // 4
    vmem = pl.BlockSpec(memory_space=pltpu.VMEM)
    return pl.pallas_call(
        functools.partial(norm_kernel, tokens=tokens),
        out_shape=(
            jax.ShapeDtypeStruct((share, feats), BF16),
            jax.ShapeDtypeStruct((share, feats), BF16),
            jax.ShapeDtypeStruct((n_t, share, basis_t.shape[0]), BF16),
        ),
        in_specs=[pl.BlockSpec(memory_space=pltpu.SMEM)] + [vmem] * 4,
        out_specs=(vmem, vmem, vmem),
        scratch_shapes=[
            pltpu.VMEM((n_z, 2, share, feats // (2 * n_z)), F32),
            pltpu.VMEM((share, feats), F32),
        ],
        compiler_params=pltpu.CompilerParams(vmem_limit_bytes=32 * 2**20),
    )(lax.axis_index("z").reshape(1), parts, norm_gain.reshape(1, feats), teacher, basis_t)


def per_device(hidden, down_weight, norm_gain, teacher, error_memory, start_basis):
    memory = error_memory[0]
    tokens, units = hidden.shape
    feats, rank = start_basis.shape
    block = down_weight.shape[1]
    n_z = lax.axis_size("z")
    n_t = lax.axis_size(TENSOR)
    share = tokens // n_t
    all_units = units * n_t

    block_t = down_weight.T
    x_other = lax.ppermute(hidden, "xl", SWAP)
    c_other = lax.ppermute(hidden, "c", SWAP)
    both = [lax.ppermute(x, "c", SWAP) for x in jnp.split(x_other, 2, axis=0)]
    up, down = [block_t], [block_t]
    for _ in range(n_z // 2 - 1):
        up.append(shift(up[-1], "z", 1))
        down.append(shift(down[-1], "z", -1))
    brought = [down[k] if k < n_z // 2 else up[n_z - k] for k in ring_order(n_z)[:-1]]
    middle = n_z // 2 - 1
    columns = [jnp.concatenate(x, axis=0) for x in (brought[:middle], brought[middle:-1])]
    near = shift(up[-1][:, : units // 2], "z", 1)
    far = shift(down[-1][:, units // 2 :], "z", -1)
    memory_term = dot(start_basis, memory, ((0,), (1,)))
    pieces = column_products((hidden, c_other), columns, (brought[-1], near, far), [x_other] + both)
    pieces = pieces.reshape(4 * n_t, share, n_z * block)
    parts = lax.all_to_all(pieces, ("xl", "c") + TENSOR, 0, 0)
    parts, memory_term = lax.optimization_barrier((parts, memory_term))

    wide_basis = jnp.pad(start_basis.T, ((0, -rank % 128), (0, 0)))
    normed, grad, probe = norm_head(parts, norm_gain, teacher, wide_basis, tokens)
    probe = lax.all_to_all(probe, TENSOR, 0, 0).reshape(tokens, -1)[:, :rank]

    term = memory_term + dot(probe, hidden, ((0,), (0,)))
    half = sum_pair_halves(term, "c", 0)
    pieces = lax.all_to_all(half.astype(BF16).reshape(2 * n_z, -1, units), ("xl", "z"), 0, 0)
    left = pair(share_out(jnp.sum(pieces.astype(F32), axis=0), ("xl", "z")).reshape(half.shape), "c")

    left2 = split_bf16(left)
    gram = dot(left, left, ((1,), (1,)), lax.Precision.HIGHEST)
    image = dot(hidden, left2, ((1,), (1,)))
    image = (image[:, :rank] + image[:, rank:]).reshape(n_t, share, rank)
    message = jnp.concatenate([image, jnp.broadcast_to(gram[None], (n_t, rank, rank))], axis=1)
    message = jnp.sum(lax.all_to_all(message, TENSOR, 0, 0), axis=0)
    image = split_bf16(message[:share].T)
    gram = message[share:]
    pulled = dot(left2, memory, ((1,), (0,)))
    right = dot(image, grad, ((1,), (0,))) + pulled
    right = right[:rank] + right[rank:]

    half = sum_pair_halves(right, "c", 0)
    pieces = lax.all_to_all(half.reshape(2 * n_t, -1, feats), ("xl",) + TENSOR, 0, 0)
    lower = lax.linalg.cholesky(gram, symmetrize_input=False)
    pieces = share_out(jnp.sum(pieces, axis=0), "z")
    inverse = lax.linalg.triangular_solve(lower, jnp.eye(rank, dtype=F32), left_side=True, lower=True)
    left_basis = dot(left, inverse, ((0,), (1,)), lax.Precision.HIGHEST) * math.sqrt(all_units)
    left_basis = left_basis.astype(BF16)
    half = share_out(jnp.sum(pieces, axis=0), ("xl",) + TENSOR).reshape(half.shape)
    right_factor = dot(pair(half, "c"), inverse, ((0,), (1,)), lax.Precision.HIGHEST)
    return normed, left_basis, right_factor.astype(BF16)


def solution(mesh):
    fine = Mesh(mesh.devices.reshape(2, 8, 2, 4, 2), DP + TENSOR)
    in_specs = (
        P(DP, TENSOR),
        P(TENSOR, DP),
        P(),
        P(DP + TENSOR, None),
        P(DP, TENSOR, None),
        P(),
    )
    out_specs = (P(DP + TENSOR, None), P(TENSOR, None), P())
    return jax.shard_map(
        per_device, mesh=fine, in_specs=in_specs, out_specs=out_specs, check_vma=False
    )
```

```python
import functools
import math

import jax
import jax.numpy as jnp
from jax import lax
from jax.experimental import pallas as pl
from jax.experimental.pallas import tpu as pltpu
from jax.sharding import Mesh
from jax.sharding import PartitionSpec as P

DP = ("xl", "z", "c")
TENSOR = ("y", "xh")
SWAP = [(0, 1), (1, 0)]
F32 = jnp.float32
BF16 = jnp.bfloat16


def dot(a, b, dims, precision=None):
    return lax.dot_general(a, b, (dims, ((), ())), precision=precision, preferred_element_type=F32)


def split_bf16(x):
    high = lax.reduce_precision(x, 8, 7)
    low = x - high
    return jnp.concatenate([high.astype(BF16), low.astype(BF16)], axis=0)


def share_out(x, axes):
    n = lax.axis_size(axes)
    return lax.all_to_all(jnp.broadcast_to(x[None], (n,) + x.shape), axes, 0, 0)


def pair(x, axis):
    other = lax.ppermute(x, axis, SWAP)
    first = lax.axis_index(axis) == 0
    return jnp.concatenate([jnp.where(first, x, other), jnp.where(first, other, x)], axis=0)


def sum_pair_halves(x, axis, dim):
    low, high = jnp.split(x, 2, axis=dim)
    first = lax.axis_index(axis) == 0
    return jnp.where(first, low, high) + lax.ppermute(jnp.where(first, high, low), axis, SWAP)


def shift(x, axis, by):
    n = lax.axis_size(axis)
    return lax.ppermute(x, axis, [(i, (i + by) % n) for i in range(n)])


def ring_order(n_z):
    return [0] + [k for far in range(1, n_z // 2) for k in (far, n_z - far)] + [n_z // 2]


def columns_kernel(me_ref, own_ref, c_ref, first_ref, second_ref, *refs):
    *sources, out_ref, x_rows, both_rows, rest, last, products, sems, out_sems = refs
    block = rest.shape[1]
    start, width = first_ref.shape[0], first_ref.shape[0] + second_ref.shape[0]
    tokens, units = own_ref.shape
    left, right = pl.ds(0, units // 2), pl.ds(units // 2, units // 2)
    targets = [rest.at[0], rest.at[1, :, left], rest.at[1, :, right]]
    targets += [x_rows]
    at = 0
    for ref in sources[4:]:
        targets.append(both_rows.at[at : at + ref.shape[0], :])
        at += ref.shape[0]
    brought = [pltpu.make_async_copy(x, y, sems.at[k]) for k, (x, y) in enumerate(zip(sources, targets))]
    for copy in brought:
        copy.start()
    sent = []

    def main(k, ref):
        products[k, :, :start] = dot(ref[...], first_ref[...], ((1,), (1,))).astype(BF16)
        products[k, :, start:width] = dot(ref[...], second_ref[...], ((1,), (1,))).astype(BF16)

    def finish(k, ref):
        products[k, :, width:] = dot(ref[...], last[...], ((1,), (1,))).astype(BF16)
        sent.append(pltpu.make_async_copy(products.at[k], out_ref.at[me_ref[0] ^ k], out_sems.at[k]))
        sent[-1].start()

    main(0, own_ref)
    for copy in brought[:3]:
        copy.wait()
    last[:block, :] = rest[0]
    last[block:, :] = rest[1]
    finish(0, own_ref)
    main(1, c_ref)
    finish(1, c_ref)
    brought[3].wait()
    main(2, x_rows)
    finish(2, x_rows)
    for copy in brought[4:]:
        copy.wait()
    main(3, both_rows)
    finish(3, both_rows)
    for copy in sent:
        copy.wait()


def column_products(rows, columns, rest, halves):
    tokens, units = rows[0].shape
    block = rest[0].shape[0]
    me = 2 * lax.axis_index("xl") + lax.axis_index("c")
    out = jax.ShapeDtypeStruct((4, tokens, sum(x.shape[0] for x in columns) + 2 * block), BF16)
    vmem = pl.BlockSpec(memory_space=pltpu.VMEM)
    hbm = pl.BlockSpec(memory_space=pltpu.HBM)
    return pl.pallas_call(
        columns_kernel,
        out_shape=out,
        in_specs=[pl.BlockSpec(memory_space=pltpu.SMEM)] + [vmem] * 4 + [hbm] * (len(rest) + len(halves)),
        out_specs=hbm,
        scratch_shapes=[
            pltpu.VMEM((tokens, units), BF16),
            pltpu.VMEM((tokens, units), BF16),
            pltpu.VMEM((2, block, units), BF16),
            pltpu.VMEM((2 * block, units), BF16),
            pltpu.VMEM(out.shape, BF16),
            pltpu.SemaphoreType.DMA((len(rest) + len(halves),)),
            pltpu.SemaphoreType.DMA((4,)),
        ],
        compiler_params=pltpu.CompilerParams(vmem_limit_bytes=24 * 2**20),
    )(me.reshape(1), *rows, *columns, *rest, *halves)


def norm_kernel(z_ref, parts_ref, gain_ref, teacher_ref, basis_ref, normed_ref, grad_ref, sent_ref, blocks, mixed_ref, *, tokens):
    n_z, _, _, two = blocks.shape
    block = two // 2
    share, feats = mixed_ref.shape
    n_t = parts_ref.shape[0] // 4
    for x in range(2):
        for c in range(2):
            total = jnp.zeros((share, n_z * block), F32)
            for t in range(n_t):
                total += parts_ref[(2 * x + c) * n_t + t].astype(F32)
            for at, k in enumerate(ring_order(n_z)):
                blocks[k, x, :, c * block : (c + 1) * block] = total[:, at * block : (at + 1) * block]
    for x in range(2):
        for z in range(n_z):
            at = (x * n_z + z) * two
            mixed_ref[:, at : at + two] = blocks[lax.rem(z - z_ref[0] + n_z, n_z), x]
    mixed = mixed_ref[...]
    gain = gain_ref[...]
    scale = lax.rsqrt(jnp.mean(mixed * mixed, axis=1, keepdims=True) + 1e-06)
    unit = mixed * scale
    normed_full = unit * gain
    normed_ref[...] = normed_full.astype(BF16)
    delta = (normed_full - teacher_ref[...].astype(F32)) * (gain / tokens)
    grad = (scale * (delta - unit * jnp.mean(delta * unit, axis=1, keepdims=True))).astype(BF16)
    grad_ref[...] = grad
    probe = dot(grad, basis_ref[...], ((1,), (1,))).astype(BF16)
    for t in range(n_t):
        sent_ref[t] = probe


def norm_head(parts, norm_gain, teacher, basis_t, tokens):
    share, feats = teacher.shape
    n_z = lax.axis_size("z")
    n_t = parts.shape[0] // 4
    vmem = pl.BlockSpec(memory_space=pltpu.VMEM)
    return pl.pallas_call(
        functools.partial(norm_kernel, tokens=tokens),
        out_shape=(
            jax.ShapeDtypeStruct((share, feats), BF16),
            jax.ShapeDtypeStruct((share, feats), BF16),
            jax.ShapeDtypeStruct((n_t, share, basis_t.shape[0]), BF16),
        ),
        in_specs=[pl.BlockSpec(memory_space=pltpu.SMEM)] + [vmem] * 4,
        out_specs=(vmem, vmem, vmem),
        scratch_shapes=[
            pltpu.VMEM((n_z, 2, share, feats // (2 * n_z)), F32),
            pltpu.VMEM((share, feats), F32),
        ],
        compiler_params=pltpu.CompilerParams(vmem_limit_bytes=32 * 2**20),
    )(lax.axis_index("z").reshape(1), parts, norm_gain.reshape(1, feats), teacher, basis_t)


def per_device(hidden, down_weight, norm_gain, teacher, error_memory, start_basis):
    memory = error_memory[0]
    tokens, units = hidden.shape
    feats, rank = start_basis.shape
    block = down_weight.shape[1]
    n_z = lax.axis_size("z")
    n_t = lax.axis_size(TENSOR)
    share = tokens // n_t
    all_units = units * n_t

    block_t = down_weight.T
    x_other = lax.ppermute(hidden, "xl", SWAP)
    c_other = lax.ppermute(hidden, "c", SWAP)
    both = [lax.ppermute(x, "c", SWAP) for x in jnp.split(x_other, 2, axis=0)]
    up, down = [block_t], [block_t]
    for _ in range(n_z // 2 - 1):
        up.append(shift(up[-1], "z", 1))
        down.append(shift(down[-1], "z", -1))
    brought = [down[k] if k < n_z // 2 else up[n_z - k] for k in ring_order(n_z)[:-1]]
    middle = n_z // 2 - 1
    columns = [jnp.concatenate(x, axis=0) for x in (brought[:middle], brought[middle:-1])]
    near = shift(up[-1][:, : units // 2], "z", 1)
    far = shift(down[-1][:, units // 2 :], "z", -1)
    memory_term = dot(start_basis, memory, ((0,), (1,)))
    pieces = column_products((hidden, c_other), columns, (brought[-1], near, far), [x_other] + both)
    pieces = pieces.reshape(4 * n_t, share, n_z * block)
    parts = lax.all_to_all(pieces, ("xl", "c") + TENSOR, 0, 0)
    parts, memory_term = lax.optimization_barrier((parts, memory_term))

    wide_basis = jnp.pad(start_basis.T, ((0, -rank % 128), (0, 0)))
    normed, grad, probe = norm_head(parts, norm_gain, teacher, wide_basis, tokens)
    probe = lax.all_to_all(probe, TENSOR, 0, 0).reshape(tokens, -1)[:, :rank]

    term = memory_term + dot(probe, hidden, ((0,), (0,)))
    half = sum_pair_halves(term, "c", 0)
    pieces = lax.all_to_all(half.astype(BF16).reshape(2 * n_z, -1, units), ("xl", "z"), 0, 0)
    left = pair(share_out(jnp.sum(pieces.astype(F32), axis=0), ("xl", "z")).reshape(half.shape), "c")

    left2 = split_bf16(left)
    gram = dot(left, left, ((1,), (1,)), lax.Precision.HIGHEST)
    image = dot(hidden, left2, ((1,), (1,)))
    image = (image[:, :rank] + image[:, rank:]).reshape(n_t, share, rank)
    message = jnp.concatenate([image, jnp.broadcast_to(gram[None], (n_t, rank, rank))], axis=1)
    message = jnp.sum(lax.all_to_all(message, TENSOR, 0, 0), axis=0)
    image = split_bf16(message[:share].T)
    gram = message[share:]
    pulled = dot(left2, memory, ((1,), (0,)))
    right = dot(image, grad, ((1,), (0,))) + pulled
    right = right[:rank] + right[rank:]

    half = sum_pair_halves(right, "c", 0)
    pieces = lax.all_to_all(half.reshape(2 * n_t, -1, feats), ("xl",) + TENSOR, 0, 0)
    lower = lax.linalg.cholesky(gram, symmetrize_input=False)
    pieces = share_out(jnp.sum(pieces, axis=0), "z")
    inverse = lax.linalg.triangular_solve(lower, jnp.eye(rank, dtype=F32), left_side=True, lower=True)
    left_basis = dot(left, inverse, ((0,), (1,)), lax.Precision.HIGH) * math.sqrt(all_units)
    left_basis = left_basis.astype(BF16)
    half = share_out(jnp.sum(pieces, axis=0), ("xl",) + TENSOR).reshape(half.shape)
    right_factor = dot(pair(half, "c"), inverse, ((0,), (1,)), lax.Precision.HIGH)
    return normed, left_basis, right_factor.astype(BF16)


def solution(mesh):
    fine = Mesh(mesh.devices.reshape(2, 8, 2, 4, 2), DP + TENSOR)
    in_specs = (
        P(DP, TENSOR),
        P(TENSOR, DP),
        P(),
        P(DP + TENSOR, None),
        P(DP, TENSOR, None),
        P(),
    )
    out_specs = (P(DP + TENSOR, None), P(TENSOR, None), P())
    return jax.shard_map(
        per_device, mesh=fine, in_specs=in_specs, out_specs=out_specs, check_vma=False
    )
```
